128 devices in a mesh: replica: 8 (over x_lo, y), fsdp: 16 (over x_hi, z, core).
Axes of the slice: x: 4 (x_hi: 2, x_lo: 2; x = x_hi * 2 + x_lo), y: 4, z: 4, core: 2. Of those that a mesh axis runs over, the one named last changes fastest.
Arguments:
- step_index: int32 [], replicated, may hold values from 1 to 63
- hidden: bfloat16 [8, 2, 1024, 6912], P('replica', None, 'fsdp'), may hold values from -6 to 6
- out_grad: bfloat16 [8, 2, 1024, 5120], P('replica', None, 'fsdp'), may hold values from -6 to 6
- weight: bfloat16 [8, 6912, 5120], P('replica', 'fsdp'), may hold values from -3 to 3
- moment: bfloat16 [8, 6912, 5120], P('replica', 'fsdp'), may hold values from -3 to 3
- second: bfloat16 [8, 6912, 5120], P('replica', 'fsdp'), may hold values from 0.0099487305 to 1
Outputs:
- new_weight: bfloat16 [8, 6912, 5120], P('replica', 'fsdp')
- new_moment: bfloat16 [8, 6912, 5120], P('replica', 'fsdp')
- hidden_grad: bfloat16 [8, 2, 1024, 6912], P('replica', None, 'fsdp')
The draws below stay inside these ranges and needn't reach their ends.
Inputs may be any that keep to these rules, and one draw needn't show every extreme that they name: `step_index`: the step index of the update; it selects the distance of the averaging partner.
All inputs are finite; a program needn't handle non-finite values.
Results may differ from the reference program's by a relative error of at most 0.0052.
Values may be sent and summed in bfloat16 or wider, within the bound.
A program may use at most 128 MiB of HBM per device.

```python
import math
import jax
import jax.numpy as jnp
from jax import lax

D = 5120
FF_WIN = 6912
MICRO = 2
REPLICAS = 8
MB_ROWS = 1024
N_REPLICA = 8


def shard_levels(stream_key, extent, pieces, smallest, top_value):
    def one(dim, shards_of):
        draws = jax.random.uniform(jax.random.fold_in(jax.random.fold_in(stream_key, 6), dim), (shards_of,), jnp.float32, smallest / len(pieces), top_value / len(pieces))
        return jnp.repeat(jnp.exp(draws), extent[dim] // shards_of).reshape((-1,) + (1,) * (len(extent) - dim - 1))

    factor_of = one(*pieces[0])
    for cut in pieces[1:]:
        factor_of = factor_of * one(*cut)
    return factor_of


def gaussian(own_key, shape, deviation, limit, split=(), kind=jnp.bfloat16):
    values = deviation * jax.random.normal(own_key, shape, jnp.float32)
    if split:
        values = values * shard_levels(own_key, shape, split, -0.22, 0.18)
    return jnp.clip(values, -limit, limit).astype(kind)


def setup_inputs(seed: int = 0) -> dict:
    splits = jax.random.split(jax.random.key(seed), 7)
    step_index = jax.random.randint(splits[0], (), 1, 64).astype(jnp.int32)
    hidden = gaussian(splits[1], (REPLICAS, MICRO, MB_ROWS, FF_WIN), 1.0, 6.0, ((0, 8), (2, 16)))
    out_grad = gaussian(splits[2], (REPLICAS, MICRO, MB_ROWS, D), 1.0, 6.0, ((0, 8), (2, 16)))
    weight = gaussian(splits[3], (REPLICAS, FF_WIN, D), 1.0, 3.0, ((0, 8), (1, 16)))
    moment = gaussian(splits[4], (REPLICAS, FF_WIN, D), 0.5, 3.0, ((0, 8), (1, 16)))
    second = jnp.clip(jnp.exp(math.log(1.0) - 4.61031033 * jax.random.uniform(splits[5], (REPLICAS, FF_WIN, D), jnp.float32) ** shard_levels(splits[5], (REPLICAS, FF_WIN, D), ((0, 8), (1, 16)), -0.2, 0.2)), 0.0099487305, 1.0).astype(jnp.bfloat16)
    return {"step_index": step_index, "hidden": hidden, "out_grad": out_grad, "weight": weight, "moment": moment, "second": second}


beta_one = 0.9
beta_two = 0.95
learn_rate = 0.05
decay_rate = 0.4
epsilon = 1e-08

def replica_step(operands, step_float):
    hidden, out_grad, weight, moment, second = operands
    factor = FF_WIN ** (-0.5)
    token_hidden = hidden.reshape(MICRO * MB_ROWS, FF_WIN)
    token_grads = out_grad.reshape(MICRO * MB_ROWS, D)
    gradient = factor * jnp.dot(token_hidden.T, token_grads, preferred_element_type=jnp.float32)
    hidden_grad = (factor * jnp.dot(token_grads, weight.T, preferred_element_type=jnp.float32)).astype(jnp.bfloat16)
    first_moment = beta_one * moment.astype(jnp.float32) + (1.0 - beta_one) * gradient
    variance = beta_two * second.astype(jnp.float32) + (1.0 - beta_two) * gradient * gradient
    bias_one = 1.0 - beta_one ** step_float
    bias_two = 1.0 - beta_two ** step_float
    update = first_moment / bias_one / (jnp.sqrt(variance / bias_two) + epsilon)
    weight_wide = weight.astype(jnp.float32)
    stepped = (weight_wide - learn_rate * (update + decay_rate * weight_wide)).astype(jnp.bfloat16)
    return (stepped, first_moment.astype(jnp.bfloat16), hidden_grad.reshape(MICRO, MB_ROWS, FF_WIN))

def reference(step_index, hidden, out_grad, weight, moment, second):
    step_float = step_index.astype(jnp.float32)
    stepped, new_moment, hidden_grad = lax.map(lambda operands: replica_step(operands, step_float), (hidden, out_grad, weight, moment, second))
    levels = N_REPLICA.bit_length() - 1
    distance = jnp.left_shift(jnp.int32(1), (step_index % levels).astype(jnp.int32))
    source = ((jnp.arange(REPLICAS, dtype=jnp.int32) - distance) % REPLICAS).astype(jnp.int32)
    partner = jnp.take(stepped, source, axis=0)
    new_weight = (0.5 * (stepped.astype(jnp.float32) + partner.astype(jnp.float32))).astype(jnp.bfloat16)
    return (new_weight, new_moment, hidden_grad)
```

```python
import functools

import jax
import jax.numpy as jnp
from jax import lax
from jax.experimental import pallas as pl
from jax.experimental.pallas import tpu as pltpu
from jax.sharding import PartitionSpec as P

beta_one = 0.9
beta_two = 0.95
learn_rate = 0.05
decay_rate = 0.4
epsilon = 1e-08

MESH = pl.DeviceIdType.MESH
GROUP = 16
REPLICAS = 8
LANES = 128
CHUNK = 256

TO_X, TO_NEXT, TO_PREV, CORE_OWN, ON_NEXT, ON_PREV, CORE_PREV, CORE_NEXT, CORE_FAR = range(9)
COPIES = 9


def slot_of(index):
    x_hi, z, core = index // 8, (index // 2) % 4, index % 2
    return z * 4 + core * 2 + x_hi


def step_kernel(
    distance,
    factor,
    scale_ref,
    hidden_hbm,
    grads_hbm,
    weight_hbm,
    moment_hbm,
    second_hbm,
    new_weight_hbm,
    new_moment_hbm,
    hidden_grad_hbm,
    gathered,
    token_hidden,
    hidden_out,
    hidden_in,
    hidden_t,
    total,
    stepped,
    partner,
    cotangent_out,
    cotangent_in,
    weight_buf,
    moment_buf,
    second_buf,
    new_moment_buf,
    new_weight_buf,
    load_sem,
    own_sem,
    param_sem,
    moment_out_sem,
    weight_out_sem,
    gather_send,
    gather_recv,
    hidden_send,
    hidden_recv,
    back_send,
    back_recv,
    gossip_send,
    gossip_recv,
):
    chunks = gathered.shape[0]
    rows = weight_buf.shape[1]
    micro, tokens = token_hidden.shape[0], token_hidden.shape[1]
    width = token_hidden.shape[2]
    unit = micro * tokens
    blocks = width // LANES

    replica = lax.axis_index("replica")
    index = lax.axis_index("fsdp")
    x_hi, z, core = index // 8, (index // 2) % 4, index % 2
    z_next, z_prev, z_far = (z + 1) % 4, (z + 3) % 4, (z + 2) % 4

    def place(x, zz, c):
        return (replica, (x * 4 + zz) * 2 + c)

    x_peer = place(1 - x_hi, z, core)
    next_peer = place(x_hi, z_next, core)
    prev_peer = place(x_hi, z_prev, core)
    core_peer = place(x_hi, z, 1 - core)
    gossip_to = ((replica + distance) % REPLICAS, index)
    gossip_from = ((replica + REPLICAS - distance) % REPLICAS, index)

    def pair_rows(zz, c):
        return pl.ds(pl.multiple_of((zz * 2 + c) * 2 * unit, 2 * unit), 2 * unit)

    def unit_rows(zz, c, x):
        return pl.ds(pl.multiple_of((zz * 4 + c * 2 + x) * unit, unit), unit)

    def chunk_columns(k):
        return pl.ds(pl.multiple_of(k * CHUNK, CHUNK), CHUNK)

    hidden_load = pltpu.make_async_copy(hidden_hbm.at[0], token_hidden, load_sem.at[0])
    hidden_load.start()

    own_start = slot_of(index) * unit

    def own_load(k, part):
        return pltpu.make_async_copy(
            grads_hbm.at[0, part, :, chunk_columns(k)],
            gathered.at[k, pl.ds(pl.multiple_of(own_start + part * tokens, tokens), tokens)],
            own_sem.at[k, part],
        )

    def start_own(k, carry):
        for part in range(micro):
            own_load(k, part).start()
        return carry

    lax.fori_loop(0, chunks, start_own, 0)

    def param_loads(k):
        slot = k % 2
        return [
            pltpu.make_async_copy(
                source.at[0, :, chunk_columns(k)], target.at[slot], param_sem.at[slot, i]
            )
            for i, (source, target) in enumerate(
                (
                    (weight_hbm, weight_buf),
                    (moment_hbm, moment_buf),
                    (second_hbm, second_buf),
                )
            )
        ]

    for load in param_loads(0):
        load.start()

    barrier = pltpu.get_barrier_semaphore()

    def greet(s, carry):
        pl.semaphore_signal(
            barrier, 1, device_id=(replica, (index + s) % GROUP), device_id_type=MESH
        )
        return carry

    lax.fori_loop(1, GROUP, greet, 0)
    pl.semaphore_signal(barrier, 1, device_id=gossip_to, device_id_type=MESH)
    pl.semaphore_signal(barrier, 1, device_id=gossip_from, device_id_type=MESH)
    pl.semaphore_wait(barrier, GROUP - 1 + 2)

    def gather_copy(k, which, where, peer):
        return pltpu.make_async_remote_copy(
            src_ref=gathered.at[k, where],
            dst_ref=gathered.at[k, where],
            send_sem=gather_send.at[k, which],
            recv_sem=gather_recv.at[k, which],
            device_id=peer,
            device_id_type=MESH,
        )

    def stage_x(k):
        for part in range(micro):
            own_load(k, part).wait()
        gather_copy(k, TO_X, unit_rows(z, core, x_hi), x_peer).start()

    def stage_pair(k):
        gather_copy(k, TO_X, unit_rows(z, core, 1 - x_hi), x_peer).wait_recv()
        gather_copy(k, TO_NEXT, pair_rows(z, core), next_peer).start()
        gather_copy(k, TO_PREV, pair_rows(z, core), prev_peer).start()
        gather_copy(k, CORE_OWN, pair_rows(z, core), core_peer).start()

    def stage_forward(k):
        gather_copy(k, TO_NEXT, pair_rows(z_prev, core), next_peer).wait_recv()
        gather_copy(k, ON_NEXT, unit_rows(z_prev, core, 0), next_peer).start()
        gather_copy(k, TO_PREV, pair_rows(z_next, core), prev_peer).wait_recv()
        gather_copy(k, ON_PREV, unit_rows(z_next, core, 1), prev_peer).start()
        gather_copy(k, CORE_PREV, pair_rows(z_prev, core), core_peer).start()
        gather_copy(k, CORE_NEXT, pair_rows(z_next, core), core_peer).start()

    def stage_far(k):
        gather_copy(k, ON_NEXT, unit_rows(z_far, core, 0), next_peer).wait_recv()
        gather_copy(k, ON_PREV, unit_rows(z_far, core, 1), prev_peer).wait_recv()
        gather_copy(k, CORE_FAR, pair_rows(z_far, core), core_peer).start()

    def stage_core(k):
        for which, zz in (
            (CORE_OWN, z),
            (CORE_PREV, z_prev),
            (CORE_NEXT, z_next),
            (CORE_FAR, z_far),
        ):
            gather_copy(k, which, pair_rows(zz, 1 - core), core_peer).wait_recv()

    stage_x(0)
    stage_x(1)

    hidden_load.wait()

    def turn(b, carry):
        lanes = pl.ds(pl.multiple_of(b * LANES, LANES), LANES)
        block = token_hidden[:, :, lanes].reshape(unit, LANES)
        hidden_out[lanes, :] = block.T
        return carry

    lax.fori_loop(0, blocks, turn, 0)

    def hidden_rows(f):
        return pl.ds(pl.multiple_of(f * rows, 16), rows)

    def hidden_copy(s):
        peer = (index + s) % GROUP
        return pltpu.make_async_remote_copy(
            src_ref=hidden_out.at[hidden_rows(peer)],
            dst_ref=hidden_in.at[slot_of(index)],
            send_sem=hidden_send.at[s],
            recv_sem=hidden_recv.at[s],
            device_id=(replica, peer),
            device_id_type=MESH,
        )

    def hidden_start(s, carry):
        hidden_copy(s).start()
        return carry

    lax.fori_loop(1, GROUP, hidden_start, 0)

    def hidden_arrived(s, carry):
        owner = (index + GROUP - s) % GROUP
        slot = slot_of(owner)
        pltpu.make_async_remote_copy(
            src_ref=hidden_out.at[hidden_rows(index)],
            dst_ref=hidden_in.at[slot],
            send_sem=hidden_send.at[s],
            recv_sem=hidden_recv.at[s],
            device_id=(replica, owner),
            device_id_type=MESH,
        ).wait_recv()
        lanes = pl.ds(pl.multiple_of(slot * unit, unit), unit)
        hidden_t[:, lanes] = hidden_in[slot]
        return carry

    def gossip_copy(k):
        return pltpu.make_async_remote_copy(
            src_ref=stepped.at[k],
            dst_ref=partner.at[k],
            send_sem=gossip_send.at[k],
            recv_sem=gossip_recv.at[k],
            device_id=gossip_to,
            device_id_type=MESH,
        )

    def moment_store(k):
        return pltpu.make_async_copy(
            new_moment_buf.at[k % 2],
            new_moment_hbm.at[0, :, chunk_columns(k)],
            moment_out_sem.at[k % 2],
        )

    def weight_store(k):
        return pltpu.make_async_copy(
            new_weight_buf.at[k % 2],
            new_weight_hbm.at[0, :, chunk_columns(k)],
            weight_out_sem.at[k % 2],
        )

    bias_one = scale_ref[0]
    bias_two = scale_ref[1]

    def update(k):
        slot = k % 2
        for load in param_loads(k):
            load.wait()

        @pl.when(k + 1 < chunks)
        def _():
            for load in param_loads(k + 1):
                load.start()

        gradient = factor * jnp.dot(
            hidden_t[...], gathered[k], preferred_element_type=jnp.float32
        )

        @pl.when(k >= 2)
        def _():
            moment_store(k - 2).wait()

        first = beta_one * moment_buf[slot].astype(jnp.float32) + (1.0 - beta_one) * gradient
        new_moment_buf[slot] = first.astype(jnp.bfloat16)
        variance = (
            beta_two * second_buf[slot].astype(jnp.float32)
            + (1.0 - beta_two) * gradient * gradient
        )
        change = first / bias_one / (jnp.sqrt(variance / bias_two) + epsilon)
        wide = weight_buf[slot].astype(jnp.float32)
        stepped[k] = (wide - learn_rate * (change + decay_rate * wide)).astype(jnp.bfloat16)
        gossip_copy(k).start()
        moment_store(k).start()

    def cotangent(k):
        slot = k % 2
        part = lax.dot_general(
            weight_buf[slot],
            gathered[k],
            (((1,), (1,)), ((), ())),
            preferred_element_type=jnp.float32,
        )
        total[...] += part

    def step(i, carry):
        @pl.when(i + 2 < chunks)
        def _():
            stage_x(i + 2)

        @pl.when(i < chunks)
        def _():
            stage_pair(i)

        @pl.when((i >= 1) & (i - 1 < chunks))
        def _():
            stage_forward(i - 1)

        @pl.when((i >= 2) & (i - 2 < chunks))
        def _():
            stage_far(i - 2)

        @pl.when(i == 3)
        def _():
            lax.fori_loop(1, GROUP, hidden_arrived, 0)
            own_lanes = pl.ds(pl.multiple_of(slot_of(index) * unit, unit), unit)
            hidden_t[:, own_lanes] = hidden_out[hidden_rows(index)]
            total[...] = jnp.zeros_like(total)

        @pl.when(i >= 3)
        def _():
            stage_core(i - 3)
            update(i - 3)
            cotangent(i - 3)

        return carry

    lax.fori_loop(0, chunks + 3, step, 0)

    def back_copy(s):
        peer = (index + s) % GROUP
        return pltpu.make_async_remote_copy(
            src_ref=cotangent_out.at[peer],
            dst_ref=cotangent_in.at[hidden_rows(index)],
            send_sem=back_send.at[s],
            recv_sem=back_recv.at[s],
            device_id=(replica, peer),
            device_id_type=MESH,
        )

    def part_of(f):
        lanes = pl.ds(pl.multiple_of(slot_of(f) * unit, unit), unit)
        return (factor * total[:, lanes]).astype(jnp.bfloat16)

    def back_start(s, carry):
        peer = (index + s) % GROUP
        cotangent_out[peer] = part_of(peer)
        back_copy(s).start()
        return carry

    lax.fori_loop(1, GROUP, back_start, 0)
    cotangent_in[hidden_rows(index)] = part_of(index)

    def average(k, carry):
        gossip_copy(k).wait_recv()

        @pl.when(k >= 2)
        def _():
            weight_store(k - 2).wait()

        mean = 0.5 * (stepped[k].astype(jnp.float32) + partner[k].astype(jnp.float32))
        new_weight_buf[k % 2] = mean.astype(jnp.bfloat16)
        weight_store(k).start()
        return carry

    late = chunks - 4
    lax.fori_loop(0, late, average, 0)

    def back_arrived(s, carry):
        owner = (index + GROUP - s) % GROUP
        pltpu.make_async_remote_copy(
            src_ref=cotangent_out.at[owner],
            dst_ref=cotangent_in.at[hidden_rows(owner)],
            send_sem=back_send.at[s],
            recv_sem=back_recv.at[s],
            device_id=(replica, owner),
            device_id_type=MESH,
        ).wait_recv()
        return carry

    lax.fori_loop(1, GROUP, back_arrived, 0)

    def turn_back(b, carry):
        lanes = pl.ds(pl.multiple_of(b * LANES, LANES), LANES)
        block = cotangent_in[lanes, :].T
        token_hidden[:, :, lanes] = block.reshape(micro, tokens, LANES)
        return carry

    lax.fori_loop(0, blocks, turn_back, 0)
    hidden_grad_store = pltpu.make_async_copy(token_hidden, hidden_grad_hbm.at[0], load_sem.at[0])
    hidden_grad_store.start()

    lax.fori_loop(late, chunks, average, 0)

    def sent(k, carry):
        gather_copy(k, TO_X, unit_rows(z, core, x_hi), x_peer).wait_send()
        gather_copy(k, TO_NEXT, pair_rows(z, core), next_peer).wait_send()
        gather_copy(k, TO_PREV, pair_rows(z, core), prev_peer).wait_send()
        gather_copy(k, CORE_OWN, pair_rows(z, core), core_peer).wait_send()
        gather_copy(k, ON_NEXT, unit_rows(z_prev, core, 0), next_peer).wait_send()
        gather_copy(k, ON_PREV, unit_rows(z_next, core, 1), prev_peer).wait_send()
        gather_copy(k, CORE_PREV, pair_rows(z_prev, core), core_peer).wait_send()
        gather_copy(k, CORE_NEXT, pair_rows(z_next, core), core_peer).wait_send()
        gather_copy(k, CORE_FAR, pair_rows(z_far, core), core_peer).wait_send()
        gossip_copy(k).wait_send()
        return carry

    lax.fori_loop(0, chunks, sent, 0)

    def exchanged(s, carry):
        hidden_copy(s).wait_send()
        back_copy(s).wait_send()
        return carry

    lax.fori_loop(1, GROUP, exchanged, 0)
    for k in (chunks - 2, chunks - 1):
        moment_store(k).wait()
        weight_store(k).wait()
    hidden_grad_store.wait()


def step_call(level, factor, scale, hidden, out_grad, weight, moment, second):
    _, micro, tokens, width = hidden.shape
    _, rows, depth = weight.shape
    chunks = depth // CHUNK
    unit = micro * tokens
    half = jnp.bfloat16
    anywhere = pl.BlockSpec(memory_space=pl.ANY)
    scratch = [
        pltpu.VMEM((chunks, GROUP * unit, CHUNK), half),
        pltpu.VMEM((micro, tokens, width), half),
        pltpu.VMEM((width, unit), half),
        pltpu.VMEM((GROUP, rows, unit), half),
        pltpu.VMEM((rows, GROUP * unit), half),
        pltpu.VMEM((rows, GROUP * unit), jnp.float32),
        pltpu.VMEM((chunks, rows, CHUNK), half),
        pltpu.VMEM((chunks, rows, CHUNK), half),
        pltpu.VMEM((GROUP, rows, unit), half),
        pltpu.VMEM((width, unit), half),
        pltpu.VMEM((2, rows, CHUNK), half),
        pltpu.VMEM((2, rows, CHUNK), half),
        pltpu.VMEM((2, rows, CHUNK), half),
        pltpu.VMEM((2, rows, CHUNK), half),
        pltpu.VMEM((2, rows, CHUNK), half),
        pltpu.SemaphoreType.DMA((1,)),
        pltpu.SemaphoreType.DMA((chunks, micro)),
        pltpu.SemaphoreType.DMA((2, 3)),
        pltpu.SemaphoreType.DMA((2,)),
        pltpu.SemaphoreType.DMA((2,)),
        pltpu.SemaphoreType.DMA((chunks, COPIES)),
        pltpu.SemaphoreType.DMA((chunks, COPIES)),
        pltpu.SemaphoreType.DMA((GROUP,)),
        pltpu.SemaphoreType.DMA((GROUP,)),
        pltpu.SemaphoreType.DMA((GROUP,)),
        pltpu.SemaphoreType.DMA((GROUP,)),
        pltpu.SemaphoreType.DMA((chunks,)),
        pltpu.SemaphoreType.DMA((chunks,)),
    ]
    products = 2 * GROUP * unit * rows * depth
    return pl.pallas_call(
        functools.partial(step_kernel, 1 << level, factor),
        out_shape=(
            jax.ShapeDtypeStruct(weight.shape, half),
            jax.ShapeDtypeStruct(moment.shape, half),
            jax.ShapeDtypeStruct(hidden.shape, half),
        ),
        in_specs=[pl.BlockSpec(memory_space=pltpu.SMEM)] + [anywhere] * 5,
        out_specs=(anywhere,) * 3,
        scratch_shapes=scratch,
        name=f"step_{1 << level}",
        cost_estimate=pl.CostEstimate(
            flops=2 * products,
            bytes_accessed=2 * (2 * hidden.size + out_grad.size + 5 * weight.size),
            transcendentals=weight.size,
        ),
        compiler_params=pltpu.CompilerParams(
            collective_id=level, has_side_effects=True, vmem_limit_bytes=60 * 2**20
        ),
    )(scale, hidden, out_grad, weight, moment, second)


def on_device(step_index, hidden, out_grad, weight, moment, second):
    factor = hidden.shape[3] ** (-0.5)
    step_float = step_index.astype(jnp.float32)
    scale = jnp.stack([1.0 - beta_one**step_float, 1.0 - beta_two**step_float])
    levels = REPLICAS.bit_length() - 1
    branches = [functools.partial(step_call, level, factor) for level in range(levels)]
    return lax.switch(
        step_index % levels, branches, scale, hidden, out_grad, weight, moment, second
    )


def solution(mesh):
    placed = (
        P(),
        P("replica", None, "fsdp", None),
        P("replica", None, "fsdp", None),
        P("replica", "fsdp", None),
        P("replica", "fsdp", None),
        P("replica", "fsdp", None),
    )
    return jax.shard_map(
        on_device,
        mesh=mesh,
        in_specs=placed,
        out_specs=(
            P("replica", "fsdp", None),
            P("replica", "fsdp", None),
            P("replica", None, "fsdp", None),
        ),
        check_vma=False,
    )
```

```python
import functools

import jax
import jax.numpy as jnp
from jax import lax
from jax.experimental import pallas as pl
from jax.experimental.pallas import tpu as pltpu
from jax.sharding import PartitionSpec as P

beta_one = 0.9
beta_two = 0.95
learn_rate = 0.05
decay_rate = 0.4
epsilon = 1e-08

MESH = pl.DeviceIdType.MESH
GROUP = 16
REPLICAS = 8
LANES = 128
CHUNK = 256
EARLY = 6
RELAY_LAG = 6
TURNS = 6

TO_X, TO_NEXT, TO_PREV, CORE_OWN, ON_NEXT, ON_PREV, CORE_PREV, CORE_NEXT, CORE_FAR = range(9)
COPIES = 9


def slot_of(index):
    x_hi, z, core = index // 8, (index // 2) % 4, index % 2
    return z * 4 + core * 2 + x_hi


def step_kernel(
    distance,
    factor,
    scale_ref,
    hidden_hbm,
    grads_hbm,
    weight_hbm,
    moment_hbm,
    second_hbm,
    new_weight_hbm,
    new_moment_hbm,
    hidden_grad_hbm,
    gathered,
    token_hidden,
    hidden_out,
    hidden_in,
    hidden_t,
    total,
    stepped,
    partner,
    cotangent_out,
    cotangent_in,
    weight_buf,
    moment_buf,
    second_buf,
    new_moment_buf,
    relayed,
    load_sem,
    own_sem,
    param_sem,
    moment_out_sem,
    weight_out_sem,
    gather_send,
    gather_recv,
    hidden_send,
    hidden_recv,
    back_send,
    back_recv,
    gossip_send,
    gossip_recv,
    relay_send,
    relay_recv,
):
    chunks = gathered.shape[0]
    rows = weight_buf.shape[1]
    micro, tokens = token_hidden.shape[0], token_hidden.shape[1]
    width = token_hidden.shape[2]
    unit = micro * tokens
    blocks = width // LANES

    replica = lax.axis_index("replica")
    index = lax.axis_index("fsdp")
    x_hi, z, core = index // 8, (index // 2) % 4, index % 2
    z_next, z_prev, z_far = (z + 1) % 4, (z + 3) % 4, (z + 2) % 4

    def place(x, zz, c):
        return (replica, (x * 4 + zz) * 2 + c)

    x_peer = place(1 - x_hi, z, core)
    next_peer = place(x_hi, z_next, core)
    prev_peer = place(x_hi, z_prev, core)
    core_peer = place(x_hi, z, 1 - core)
    gossip_to = ((replica + distance) % REPLICAS, index)
    gossip_from = ((replica + REPLICAS - distance) % REPLICAS, index)

    x_lo, y = replica // 4, replica % 4
    relays = relayed.shape[0] if distance < 4 else 0
    wraps = y >= 4 - distance
    lands = y < distance
    y_ahead = (x_lo * 4 + (y + distance) % 4, index)
    y_behind = (x_lo * 4 + (y + 4 - distance) % 4, index)
    x_beside = ((1 - x_lo) * 4 + y, index)

    def pair_rows(zz, c):
        return pl.ds(pl.multiple_of((zz * 2 + c) * 2 * unit, 2 * unit), 2 * unit)

    def unit_rows(zz, c, x):
        return pl.ds(pl.multiple_of((zz * 4 + c * 2 + x) * unit, unit), unit)

    def chunk_columns(k):
        return pl.ds(pl.multiple_of(k * CHUNK, CHUNK), CHUNK)

    hidden_load = pltpu.make_async_copy(hidden_hbm.at[0], token_hidden, load_sem.at[0])
    hidden_load.start()

    own_start = slot_of(index) * unit

    def own_load(k, part):
        return pltpu.make_async_copy(
            grads_hbm.at[0, part, :, chunk_columns(k)],
            gathered.at[k, pl.ds(pl.multiple_of(own_start + part * tokens, tokens), tokens)],
            own_sem.at[k, part],
        )

    def start_own(k, carry):
        for part in range(micro):
            own_load(k, part).start()
        return carry

    lax.fori_loop(0, chunks, start_own, 0)

    def param_loads(k):
        slot = k % 2
        return [
            pltpu.make_async_copy(
                source.at[0, :, chunk_columns(k)], target.at[slot], param_sem.at[slot, i]
            )
            for i, (source, target) in enumerate(
                (
                    (weight_hbm, weight_buf),
                    (moment_hbm, moment_buf),
                    (second_hbm, second_buf),
                )
            )
        ]

    for load in param_loads(0):
        load.start()

    barrier = pltpu.get_barrier_semaphore()

    def greet(s, carry):
        pl.semaphore_signal(
            barrier, 1, device_id=(replica, (index + s) % GROUP), device_id_type=MESH
        )
        return carry

    lax.fori_loop(1, GROUP, greet, 0)
    pl.semaphore_signal(barrier, 1, device_id=gossip_to, device_id_type=MESH)
    pl.semaphore_signal(barrier, 1, device_id=gossip_from, device_id_type=MESH)
    greeted = GROUP - 1 + 2
    if relays:
        for peer in (y_ahead, y_behind, x_beside):
            pl.semaphore_signal(barrier, 1, device_id=peer, device_id_type=MESH)
        greeted += 3
    pl.semaphore_wait(barrier, greeted)

    def gather_copy(k, which, where, peer):
        return pltpu.make_async_remote_copy(
            src_ref=gathered.at[k, where],
            dst_ref=gathered.at[k, where],
            send_sem=gather_send.at[k, which],
            recv_sem=gather_recv.at[k, which],
            device_id=peer,
            device_id_type=MESH,
        )

    def stage_x(k):
        for part in range(micro):
            own_load(k, part).wait()
        gather_copy(k, TO_X, unit_rows(z, core, x_hi), x_peer).start()

    def stage_pair(k):
        gather_copy(k, TO_X, unit_rows(z, core, 1 - x_hi), x_peer).wait_recv()
        gather_copy(k, TO_NEXT, pair_rows(z, core), next_peer).start()
        gather_copy(k, TO_PREV, pair_rows(z, core), prev_peer).start()
        gather_copy(k, CORE_OWN, pair_rows(z, core), core_peer).start()

    def stage_forward(k):
        gather_copy(k, TO_NEXT, pair_rows(z_prev, core), next_peer).wait_recv()
        gather_copy(k, ON_NEXT, unit_rows(z_prev, core, 0), next_peer).start()
        gather_copy(k, TO_PREV, pair_rows(z_next, core), prev_peer).wait_recv()
        gather_copy(k, ON_PREV, unit_rows(z_next, core, 1), prev_peer).start()
        gather_copy(k, CORE_PREV, pair_rows(z_prev, core), core_peer).start()
        gather_copy(k, CORE_NEXT, pair_rows(z_next, core), core_peer).start()

    def stage_far(k):
        gather_copy(k, ON_NEXT, unit_rows(z_far, core, 0), next_peer).wait_recv()
        gather_copy(k, ON_PREV, unit_rows(z_far, core, 1), prev_peer).wait_recv()
        gather_copy(k, CORE_FAR, pair_rows(z_far, core), core_peer).start()

    def stage_core(k):
        for which, zz in (
            (CORE_OWN, z),
            (CORE_PREV, z_prev),
            (CORE_NEXT, z_next),
            (CORE_FAR, z_far),
        ):
            gather_copy(k, which, pair_rows(zz, 1 - core), core_peer).wait_recv()

    stage_x(0)
    stage_x(1)

    hidden_load.wait()

    def turn(b, carry):
        for t in range(TURNS):
            lanes = pl.ds(pl.multiple_of((b * TURNS + t) * LANES, LANES), LANES)
            block = token_hidden[:, :, lanes].reshape(unit, LANES)
            hidden_out[lanes, :] = block.T
        return carry

    lax.fori_loop(0, blocks // TURNS, turn, 0)

    def hidden_rows(f):
        return pl.ds(pl.multiple_of(f * rows, 16), rows)

    def hidden_copy(s):
        peer = (index + s) % GROUP
        return pltpu.make_async_remote_copy(
            src_ref=hidden_out.at[hidden_rows(peer)],
            dst_ref=hidden_in.at[slot_of(index)],
            send_sem=hidden_send.at[s],
            recv_sem=hidden_recv.at[s],
            device_id=(replica, peer),
            device_id_type=MESH,
        )

    def hidden_start(s, carry):
        hidden_copy(s).start()
        return carry

    lax.fori_loop(1, GROUP, hidden_start, 0)

    def exchange(k, carry):
        stage_x(k)
        return carry

    lax.fori_loop(2, EARLY, exchange, 0)

    def hidden_arrived(s, carry):
        owner = (index + GROUP - s) % GROUP
        slot = slot_of(owner)
        pltpu.make_async_remote_copy(
            src_ref=hidden_out.at[hidden_rows(index)],
            dst_ref=hidden_in.at[slot],
            send_sem=hidden_send.at[s],
            recv_sem=hidden_recv.at[s],
            device_id=(replica, owner),
            device_id_type=MESH,
        ).wait_recv()
        lanes = pl.ds(pl.multiple_of(slot * unit, unit), unit)
        hidden_t[:, lanes] = hidden_in[slot]
        return carry

    def gossip_copy(k):
        return pltpu.make_async_remote_copy(
            src_ref=stepped.at[k],
            dst_ref=partner.at[k],
            send_sem=gossip_send.at[k],
            recv_sem=gossip_recv.at[k],
            device_id=gossip_to,
            device_id_type=MESH,
        )

    def relay_copy(k, peer):
        return pltpu.make_async_remote_copy(
            src_ref=stepped.at[k],
            dst_ref=relayed.at[k // 2],
            send_sem=gossip_send.at[k],
            recv_sem=relay_recv.at[k // 2],
            device_id=peer,
            device_id_type=MESH,
        )

    def pass_on_copy(k, peer):
        return pltpu.make_async_remote_copy(
            src_ref=relayed.at[k // 2],
            dst_ref=partner.at[k],
            send_sem=relay_send.at[k // 2],
            recv_sem=gossip_recv.at[k],
            device_id=peer,
            device_id_type=MESH,
        )

    def gossip_start(k):
        if relays:
            by_relay = wraps & (k // 2 < relays)

            @pl.when(by_relay & (k % 2 == 0))
            def _():
                relay_copy(k, y_ahead).start()

            @pl.when(by_relay & (k % 2 == 1))
            def _():
                relay_copy(k, x_beside).start()

            @pl.when(jnp.logical_not(by_relay))
            def _():
                gossip_copy(k).start()

        else:
            gossip_copy(k).start()

    def moment_store(k):
        return pltpu.make_async_copy(
            new_moment_buf.at[k % 2],
            new_moment_hbm.at[0, :, chunk_columns(k)],
            moment_out_sem.at[k % 2],
        )

    def weight_store(k):
        return pltpu.make_async_copy(
            partner.at[k],
            new_weight_hbm.at[0, :, chunk_columns(k)],
            weight_out_sem.at[k],
        )

    bias_one = scale_ref[0]
    bias_two = scale_ref[1]

    def update(k):
        slot = k % 2
        for load in param_loads(k):
            load.wait()

        @pl.when(k + 1 < chunks)
        def _():
            for load in param_loads(k + 1):
                load.start()

        gradient = factor * jnp.dot(
            hidden_t[...], gathered[k], preferred_element_type=jnp.float32
        )

        @pl.when(k >= 2)
        def _():
            moment_store(k - 2).wait()

        first = beta_one * moment_buf[slot].astype(jnp.float32) + (1.0 - beta_one) * gradient
        new_moment_buf[slot] = first.astype(jnp.bfloat16)
        variance = (
            beta_two * second_buf[slot].astype(jnp.float32)
            + (1.0 - beta_two) * gradient * gradient
        )
        change = first / bias_one / (jnp.sqrt(variance / bias_two) + epsilon)
        wide = weight_buf[slot].astype(jnp.float32)
        stepped[k] = (wide - learn_rate * (change + decay_rate * wide)).astype(jnp.bfloat16)
        gossip_start(k)
        moment_store(k).start()

    def cotangent(k):
        slot = k % 2
        part = lax.dot_general(
            weight_buf[slot],
            gathered[k],
            (((1,), (1,)), ((), ())),
            preferred_element_type=jnp.float32,
        )
        total[...] += part

    def step(i, carry):
        @pl.when(i < chunks)
        def _():
            stage_pair(i)

        @pl.when((i >= 1) & (i - 1 < chunks))
        def _():
            stage_forward(i - 1)

        @pl.when((i >= 2) & (i - 2 < chunks))
        def _():
            stage_far(i - 2)

        @pl.when(i == 3)
        def _():
            lax.fori_loop(1, GROUP, hidden_arrived, 0)
            own_lanes = pl.ds(pl.multiple_of(slot_of(index) * unit, unit), unit)
            hidden_t[:, own_lanes] = hidden_out[hidden_rows(index)]
            total[...] = jnp.zeros_like(total)
            lax.fori_loop(EARLY, chunks, exchange, 0)

        @pl.when((i >= 3) & (i - 3 < chunks))
        def _():
            stage_core(i - 3)
            update(i - 3)
            cotangent(i - 3)

        if relays:
            late = i - RELAY_LAG

            @pl.when(lands & (late >= 0) & (late % 2 == 0) & (late // 2 < relays))
            def _():
                relay_copy(late, x_beside).wait_recv()
                pass_on_copy(late, x_beside).start()

            @pl.when(wraps & (late >= 0) & (late % 2 == 1) & (late // 2 < relays))
            def _():
                relay_copy(late, x_beside).wait_recv()
                pass_on_copy(late, y_ahead).start()

        return carry

    lax.fori_loop(0, chunks + 4, step, 0)

    def back_copy(s):
        peer = (index + s) % GROUP
        return pltpu.make_async_remote_copy(
            src_ref=cotangent_out.at[peer],
            dst_ref=cotangent_in.at[hidden_rows(index)],
            send_sem=back_send.at[s],
            recv_sem=back_recv.at[s],
            device_id=(replica, peer),
            device_id_type=MESH,
        )

    def part_of(f):
        lanes = pl.ds(pl.multiple_of(slot_of(f) * unit, unit), unit)
        return (factor * total[:, lanes]).astype(jnp.bfloat16)

    def back_start(s, carry):
        peer = (index + s) % GROUP
        cotangent_out[peer] = part_of(peer)
        back_copy(s).start()
        return carry

    lax.fori_loop(1, GROUP, back_start, 0)
    cotangent_in[hidden_rows(index)] = part_of(index)

    def average(k, carry):
        gossip_copy(k).wait_recv()
        mean = 0.5 * (stepped[k].astype(jnp.float32) + partner[k].astype(jnp.float32))
        partner[k] = mean.astype(jnp.bfloat16)
        weight_store(k).start()
        return carry

    late = chunks - 4
    lax.fori_loop(0, late, average, 0)

    def back_arrived(s, carry):
        owner = (index + GROUP - s) % GROUP
        pltpu.make_async_remote_copy(
            src_ref=cotangent_out.at[owner],
            dst_ref=cotangent_in.at[hidden_rows(owner)],
            send_sem=back_send.at[s],
            recv_sem=back_recv.at[s],
            device_id=(replica, owner),
            device_id_type=MESH,
        ).wait_recv()
        return carry

    lax.fori_loop(1, GROUP, back_arrived, 0)

    def turn_back(b, carry):
        for t in range(TURNS):
            lanes = pl.ds(pl.multiple_of((b * TURNS + t) * LANES, LANES), LANES)
            block = cotangent_in[lanes, :].T
            token_hidden[:, :, lanes] = block.reshape(micro, tokens, LANES)
        return carry

    lax.fori_loop(0, blocks // TURNS, turn_back, 0)
    hidden_grad_store = pltpu.make_async_copy(token_hidden, hidden_grad_hbm.at[0], load_sem.at[0])
    hidden_grad_store.start()

    lax.fori_loop(late, chunks, average, 0)

    def sent(k, carry):
        gather_copy(k, TO_X, unit_rows(z, core, x_hi), x_peer).wait_send()
        gather_copy(k, TO_NEXT, pair_rows(z, core), next_peer).wait_send()
        gather_copy(k, TO_PREV, pair_rows(z, core), prev_peer).wait_send()
        gather_copy(k, CORE_OWN, pair_rows(z, core), core_peer).wait_send()
        gather_copy(k, ON_NEXT, unit_rows(z_prev, core, 0), next_peer).wait_send()
        gather_copy(k, ON_PREV, unit_rows(z_next, core, 1), prev_peer).wait_send()
        gather_copy(k, CORE_PREV, pair_rows(z_prev, core), core_peer).wait_send()
        gather_copy(k, CORE_NEXT, pair_rows(z_next, core), core_peer).wait_send()
        gather_copy(k, CORE_FAR, pair_rows(z_far, core), core_peer).wait_send()
        gossip_copy(k).wait_send()
        weight_store(k).wait()
        return carry

    lax.fori_loop(0, chunks, sent, 0)

    def exchanged(s, carry):
        hidden_copy(s).wait_send()
        back_copy(s).wait_send()
        return carry

    lax.fori_loop(1, GROUP, exchanged, 0)
    for k in (chunks - 2, chunks - 1):
        moment_store(k).wait()
    if relays:

        @pl.when(lands | wraps)
        def _():
            def passed(j, carry):
                pass_on_copy(2 * j, x_beside).wait_send()
                return carry

            lax.fori_loop(0, relays, passed, 0)

    hidden_grad_store.wait()


def step_call(level, factor, scale, hidden, out_grad, weight, moment, second):
    _, micro, tokens, width = hidden.shape
    _, rows, depth = weight.shape
    chunks = depth // CHUNK
    unit = micro * tokens
    relays = chunks // 2 - 1
    half = jnp.bfloat16
    anywhere = pl.BlockSpec(memory_space=pl.ANY)
    scratch = [
        pltpu.VMEM((chunks, GROUP * unit, CHUNK), half),
        pltpu.VMEM((micro, tokens, width), half),
        pltpu.VMEM((width, unit), half),
        pltpu.VMEM((GROUP, rows, unit), half),
        pltpu.VMEM((rows, GROUP * unit), half),
        pltpu.VMEM((rows, GROUP * unit), jnp.float32),
        pltpu.VMEM((chunks, rows, CHUNK), half),
        pltpu.VMEM((chunks, rows, CHUNK), half),
        pltpu.VMEM((GROUP, rows, unit), half),
        pltpu.VMEM((width, unit), half),
        pltpu.VMEM((2, rows, CHUNK), half),
        pltpu.VMEM((2, rows, CHUNK), half),
        pltpu.VMEM((2, rows, CHUNK), half),
        pltpu.VMEM((2, rows, CHUNK), half),
        pltpu.VMEM((relays, rows, CHUNK), half),
        pltpu.SemaphoreType.DMA((1,)),
        pltpu.SemaphoreType.DMA((chunks, micro)),
        pltpu.SemaphoreType.DMA((2, 3)),
        pltpu.SemaphoreType.DMA((2,)),
        pltpu.SemaphoreType.DMA((chunks,)),
        pltpu.SemaphoreType.DMA((chunks, COPIES)),
        pltpu.SemaphoreType.DMA((chunks, COPIES)),
        pltpu.SemaphoreType.DMA((GROUP,)),
        pltpu.SemaphoreType.DMA((GROUP,)),
        pltpu.SemaphoreType.DMA((GROUP,)),
        pltpu.SemaphoreType.DMA((GROUP,)),
        pltpu.SemaphoreType.DMA((chunks,)),
        pltpu.SemaphoreType.DMA((chunks,)),
        pltpu.SemaphoreType.DMA((relays,)),
        pltpu.SemaphoreType.DMA((relays,)),
    ]
    products = 2 * GROUP * unit * rows * depth
    return pl.pallas_call(
        functools.partial(step_kernel, 1 << level, factor),
        out_shape=(
            jax.ShapeDtypeStruct(weight.shape, half),
            jax.ShapeDtypeStruct(moment.shape, half),
            jax.ShapeDtypeStruct(hidden.shape, half),
        ),
        in_specs=[pl.BlockSpec(memory_space=pltpu.SMEM)] + [anywhere] * 5,
        out_specs=(anywhere,) * 3,
        scratch_shapes=scratch,
        name=f"step_{1 << level}",
        cost_estimate=pl.CostEstimate(
            flops=2 * products,
            bytes_accessed=2 * (2 * hidden.size + out_grad.size + 5 * weight.size),
            transcendentals=weight.size,
        ),
        compiler_params=pltpu.CompilerParams(
            collective_id=level, has_side_effects=True, vmem_limit_bytes=50 * 2**20
        ),
    )(scale, hidden, out_grad, weight, moment, second)


def on_device(step_index, hidden, out_grad, weight, moment, second):
    factor = hidden.shape[3] ** (-0.5)
    step_float = step_index.astype(jnp.float32)
    scale = jnp.stack([1.0 - beta_one**step_float, 1.0 - beta_two**step_float])
    levels = REPLICAS.bit_length() - 1
    branches = [functools.partial(step_call, level, factor) for level in range(levels)]
    return lax.switch(
        step_index % levels, branches, scale, hidden, out_grad, weight, moment, second
    )


def solution(mesh):
    placed = (
        P(),
        P("replica", None, "fsdp", None),
        P("replica", None, "fsdp", None),
        P("replica", "fsdp", None),
        P("replica", "fsdp", None),
        P("replica", "fsdp", None),
    )
    return jax.shard_map(
        on_device,
        mesh=mesh,
        in_specs=placed,
        out_specs=(
            P("replica", "fsdp", None),
            P("replica", "fsdp", None),
            P("replica", None, "fsdp", None),
        ),
        check_vma=False,
    )
```

```python
import functools

import jax
import jax.numpy as jnp
from jax import lax
from jax.experimental import pallas as pl
from jax.experimental.pallas import tpu as pltpu
from jax.sharding import PartitionSpec as P

beta_one = 0.9
beta_two = 0.95
learn_rate = 0.05
decay_rate = 0.4
epsilon = 1e-08

MESH = pl.DeviceIdType.MESH
GROUP = 16
REPLICAS = 8
LANES = 128
CHUNK = 256
EARLY = 8
FORWARD, FAR, USE, RELAY = 2, 4, 5, 8
TURNS = 6

TO_X, TO_NEXT, TO_PREV, CORE_OWN, ON_NEXT, ON_PREV, CORE_PREV, CORE_NEXT, CORE_FAR = range(9)
COPIES = 9


def slot_of(index):
    x_hi, z, core = index // 8, (index // 2) % 4, index % 2
    return z * 4 + core * 2 + x_hi


def step_kernel(
    distance,
    factor,
    scale_ref,
    hidden_hbm,
    grads_hbm,
    weight_hbm,
    moment_hbm,
    second_hbm,
    new_weight_hbm,
    new_moment_hbm,
    hidden_grad_hbm,
    gathered,
    token_hidden,
    hidden_out,
    hidden_in,
    hidden_t,
    total,
    stepped,
    partner,
    cotangent_out,
    cotangent_in,
    weight_buf,
    moment_buf,
    second_buf,
    new_moment_buf,
    relayed,
    load_sem,
    own_sem,
    param_sem,
    moment_out_sem,
    weight_out_sem,
    gather_send,
    gather_recv,
    hidden_send,
    hidden_recv,
    back_send,
    back_recv,
    gossip_send,
    gossip_recv,
    relay_send,
    relay_recv,
):
    chunks = gathered.shape[0]
    rows = weight_buf.shape[1]
    micro, tokens = token_hidden.shape[0], token_hidden.shape[1]
    width = token_hidden.shape[2]
    unit = micro * tokens
    blocks = width // LANES

    replica = lax.axis_index("replica")
    index = lax.axis_index("fsdp")
    x_hi, z, core = index // 8, (index // 2) % 4, index % 2
    z_next, z_prev, z_far = (z + 1) % 4, (z + 3) % 4, (z + 2) % 4

    def place(x, zz, c):
        return (replica, (x * 4 + zz) * 2 + c)

    x_peer = place(1 - x_hi, z, core)
    next_peer = place(x_hi, z_next, core)
    prev_peer = place(x_hi, z_prev, core)
    core_peer = place(x_hi, z, 1 - core)
    gossip_to = ((replica + distance) % REPLICAS, index)
    gossip_from = ((replica + REPLICAS - distance) % REPLICAS, index)

    x_lo, y = replica // 4, replica % 4
    relays = relayed.shape[0] if distance < 4 else 0
    wraps = y >= 4 - distance
    lands = y < distance
    y_ahead = (x_lo * 4 + (y + distance) % 4, index)
    y_behind = (x_lo * 4 + (y + 4 - distance) % 4, index)
    x_beside = ((1 - x_lo) * 4 + y, index)

    def pair_rows(zz, c):
        return pl.ds(pl.multiple_of((zz * 2 + c) * 2 * unit, 2 * unit), 2 * unit)

    def unit_rows(zz, c, x):
        return pl.ds(pl.multiple_of((zz * 4 + c * 2 + x) * unit, unit), unit)

    def chunk_columns(k):
        return pl.ds(pl.multiple_of(k * CHUNK, CHUNK), CHUNK)

    hidden_load = pltpu.make_async_copy(hidden_hbm.at[0], token_hidden, load_sem.at[0])
    hidden_load.start()

    own_start = slot_of(index) * unit

    def own_load(k, part):
        return pltpu.make_async_copy(
            grads_hbm.at[0, part, :, chunk_columns(k)],
            gathered.at[k, pl.ds(pl.multiple_of(own_start + part * tokens, tokens), tokens)],
            own_sem.at[k, part],
        )

    def start_own(k, carry):
        for part in range(micro):
            own_load(k, part).start()
        return carry

    lax.fori_loop(0, chunks, start_own, 0)

    def param_loads(k):
        slot = k % 2
        return [
            pltpu.make_async_copy(
                source.at[0, :, chunk_columns(k)], target.at[slot], param_sem.at[slot, i]
            )
            for i, (source, target) in enumerate(
                (
                    (weight_hbm, weight_buf),
                    (moment_hbm, moment_buf),
                    (second_hbm, second_buf),
                )
            )
        ]

    for load in param_loads(0):
        load.start()

    barrier = pltpu.get_barrier_semaphore()

    def greet(s, carry):
        pl.semaphore_signal(
            barrier, 1, device_id=(replica, (index + s) % GROUP), device_id_type=MESH
        )
        return carry

    lax.fori_loop(1, GROUP, greet, 0)
    pl.semaphore_signal(barrier, 1, device_id=gossip_to, device_id_type=MESH)
    pl.semaphore_signal(barrier, 1, device_id=gossip_from, device_id_type=MESH)
    greeted = GROUP - 1 + 2
    if relays:
        for peer in (y_ahead, y_behind, x_beside):
            pl.semaphore_signal(barrier, 1, device_id=peer, device_id_type=MESH)
        greeted += 3
    pl.semaphore_wait(barrier, greeted)

    def gather_copy(k, which, where, peer):
        return pltpu.make_async_remote_copy(
            src_ref=gathered.at[k, where],
            dst_ref=gathered.at[k, where],
            send_sem=gather_send.at[k, which],
            recv_sem=gather_recv.at[k, which],
            device_id=peer,
            device_id_type=MESH,
        )

    def stage_x(k):
        for part in range(micro):
            own_load(k, part).wait()
        gather_copy(k, TO_X, unit_rows(z, core, x_hi), x_peer).start()

    def stage_pair(k):
        gather_copy(k, TO_X, unit_rows(z, core, 1 - x_hi), x_peer).wait_recv()
        gather_copy(k, TO_NEXT, pair_rows(z, core), next_peer).start()
        gather_copy(k, TO_PREV, pair_rows(z, core), prev_peer).start()
        gather_copy(k, CORE_OWN, pair_rows(z, core), core_peer).start()

    def stage_forward(k):
        gather_copy(k, TO_NEXT, pair_rows(z_prev, core), next_peer).wait_recv()
        gather_copy(k, ON_NEXT, unit_rows(z_prev, core, 0), next_peer).start()
        gather_copy(k, TO_PREV, pair_rows(z_next, core), prev_peer).wait_recv()
        gather_copy(k, ON_PREV, unit_rows(z_next, core, 1), prev_peer).start()
        gather_copy(k, CORE_PREV, pair_rows(z_prev, core), core_peer).start()
        gather_copy(k, CORE_NEXT, pair_rows(z_next, core), core_peer).start()

    def stage_far(k):
        gather_copy(k, ON_NEXT, unit_rows(z_far, core, 0), next_peer).wait_recv()
        gather_copy(k, ON_PREV, unit_rows(z_far, core, 1), prev_peer).wait_recv()
        gather_copy(k, CORE_FAR, pair_rows(z_far, core), core_peer).start()

    def stage_core(k):
        for which, zz in (
            (CORE_OWN, z),
            (CORE_PREV, z_prev),
            (CORE_NEXT, z_next),
            (CORE_FAR, z_far),
        ):
            gather_copy(k, which, pair_rows(zz, 1 - core), core_peer).wait_recv()

    stage_x(0)
    stage_x(1)

    hidden_load.wait()

    def turn(b, carry):
        for t in range(TURNS):
            lanes = pl.ds(pl.multiple_of((b * TURNS + t) * LANES, LANES), LANES)
            block = token_hidden[:, :, lanes].reshape(unit, LANES)
            hidden_out[lanes, :] = block.T
        return carry

    lax.fori_loop(0, blocks // TURNS, turn, 0)

    def ahead(s):
        return ((x_hi + s // 8) % 2 * 4 + (z + (s // 2) % 4) % 4) * 2 + (core + s) % 2

    def behind(s):
        return ((x_hi + s // 8) % 2 * 4 + (z + 4 - (s // 2) % 4) % 4) * 2 + (core + s) % 2

    def hidden_rows(f):
        return pl.ds(pl.multiple_of(f * rows, 16), rows)

    def hidden_copy(s):
        peer = ahead(s)
        return pltpu.make_async_remote_copy(
            src_ref=hidden_out.at[hidden_rows(peer)],
            dst_ref=hidden_in.at[slot_of(index)],
            send_sem=hidden_send.at[s],
            recv_sem=hidden_recv.at[s],
            device_id=(replica, peer),
            device_id_type=MESH,
        )

    def hidden_start(s, carry):
        hidden_copy(GROUP - s).start()
        return carry

    lax.fori_loop(1, GROUP, hidden_start, 0)

    def exchange(k, carry):
        stage_x(k)
        return carry

    lax.fori_loop(2, EARLY, exchange, 0)

    def hidden_arrived(s, carry):
        owner = behind(s)
        slot = slot_of(owner)
        pltpu.make_async_remote_copy(
            src_ref=hidden_out.at[hidden_rows(index)],
            dst_ref=hidden_in.at[slot],
            send_sem=hidden_send.at[s],
            recv_sem=hidden_recv.at[s],
            device_id=(replica, owner),
            device_id_type=MESH,
        ).wait_recv()
        lanes = pl.ds(pl.multiple_of(slot * unit, unit), unit)
        hidden_t[:, lanes] = hidden_in[slot]
        return carry

    def gossip_copy(k):
        return pltpu.make_async_remote_copy(
            src_ref=stepped.at[k],
            dst_ref=partner.at[k],
            send_sem=gossip_send.at[k],
            recv_sem=gossip_recv.at[k],
            device_id=gossip_to,
            device_id_type=MESH,
        )

    def relay_copy(k, peer):
        return pltpu.make_async_remote_copy(
            src_ref=stepped.at[k],
            dst_ref=relayed.at[k % relays],
            send_sem=gossip_send.at[k],
            recv_sem=relay_recv.at[k % relays],
            device_id=peer,
            device_id_type=MESH,
        )

    def pass_on_copy(k, peer):
        return pltpu.make_async_remote_copy(
            src_ref=relayed.at[k % relays],
            dst_ref=partner.at[k],
            send_sem=relay_send.at[k % relays],
            recv_sem=gossip_recv.at[k],
            device_id=peer,
            device_id_type=MESH,
        )

    def pass_on(k, peer):
        relay_copy(k, x_beside).wait_recv()
        pass_on_copy(k, peer).start()

    def gossip_start(k):
        if relays:

            @pl.when(wraps & (k < relays))
            def _():
                relay_copy(k, y_ahead).start()

            @pl.when(wraps & (k >= relays))
            def _():
                relay_copy(k, x_beside).start()

            @pl.when(jnp.logical_not(wraps))
            def _():
                gossip_copy(k).start()

        else:
            gossip_copy(k).start()

    def moment_store(k):
        return pltpu.make_async_copy(
            new_moment_buf.at[k % 2],
            new_moment_hbm.at[0, :, chunk_columns(k)],
            moment_out_sem.at[k % 2],
        )

    def weight_store(k):
        return pltpu.make_async_copy(
            partner.at[k],
            new_weight_hbm.at[0, :, chunk_columns(k)],
            weight_out_sem.at[k],
        )

    bias_one = scale_ref[0]
    bias_two = scale_ref[1]

    def update(k):
        slot = k % 2
        for load in param_loads(k):
            load.wait()

        @pl.when(k + 1 < chunks)
        def _():
            for load in param_loads(k + 1):
                load.start()

        gradient = factor * jnp.dot(
            hidden_t[...], gathered[k], preferred_element_type=jnp.float32
        )

        @pl.when(k >= 2)
        def _():
            moment_store(k - 2).wait()

        first = beta_one * moment_buf[slot].astype(jnp.float32) + (1.0 - beta_one) * gradient
        new_moment_buf[slot] = first.astype(jnp.bfloat16)
        variance = (
            beta_two * second_buf[slot].astype(jnp.float32)
            + (1.0 - beta_two) * gradient * gradient
        )
        change = first / bias_one / (jnp.sqrt(variance / bias_two) + epsilon)
        wide = weight_buf[slot].astype(jnp.float32)
        stepped[k] = (wide - learn_rate * (change + decay_rate * wide)).astype(jnp.bfloat16)
        gossip_start(k)
        moment_store(k).start()

    def cotangent(k):
        slot = k % 2
        part = lax.dot_general(
            weight_buf[slot],
            gathered[k],
            (((1,), (1,)), ((), ())),
            preferred_element_type=jnp.float32,
        )
        total[...] += part

    def step(i, carry):
        @pl.when(i < chunks)
        def _():
            stage_pair(i)

        @pl.when((i >= FORWARD) & (i - FORWARD < chunks))
        def _():
            stage_forward(i - FORWARD)

        @pl.when(i == USE)
        def _():
            lax.fori_loop(1, GROUP, hidden_arrived, 0)
            own_lanes = pl.ds(pl.multiple_of(slot_of(index) * unit, unit), unit)
            hidden_t[:, own_lanes] = hidden_out[hidden_rows(index)]
            total[...] = jnp.zeros_like(total)
            lax.fori_loop(EARLY, chunks, exchange, 0)

        @pl.when((i >= USE) & (i - USE < chunks))
        def _():
            stage_core(i - USE)
            update(i - USE)

        @pl.when((i >= FAR) & (i - FAR < chunks))
        def _():
            stage_far(i - FAR)

        @pl.when((i >= USE) & (i - USE < chunks))
        def _():
            cotangent(i - USE)

        if relays:
            over_y, over_x = i - RELAY, i - USE - 1

            @pl.when(lands & (over_y >= 0) & (over_y < relays))
            def _():
                pass_on(over_y, x_beside)

            @pl.when(wraps & (over_x >= relays))
            def _():
                pass_on(over_x, y_ahead)

        return carry

    lax.fori_loop(0, chunks + USE, step, 0)

    def back_copy(s):
        peer = ahead(s)
        return pltpu.make_async_remote_copy(
            src_ref=cotangent_out.at[peer],
            dst_ref=cotangent_in.at[hidden_rows(index)],
            send_sem=back_send.at[s],
            recv_sem=back_recv.at[s],
            device_id=(replica, peer),
            device_id_type=MESH,
        )

    def part_of(f):
        lanes = pl.ds(pl.multiple_of(slot_of(f) * unit, unit), unit)
        return (factor * total[:, lanes]).astype(jnp.bfloat16)

    def back_start(s, carry):
        peer = ahead(GROUP - s)
        cotangent_out[peer] = part_of(peer)
        back_copy(GROUP - s).start()
        return carry

    lax.fori_loop(1, GROUP, back_start, 0)
    cotangent_in[hidden_rows(index)] = part_of(index)
    if relays:

        @pl.when(wraps)
        def _():
            pass_on(chunks - 1, y_ahead)


    def average(k, carry):
        gossip_copy(k).wait_recv()
        mean = 0.5 * (stepped[k].astype(jnp.float32) + partner[k].astype(jnp.float32))
        partner[k] = mean.astype(jnp.bfloat16)
        weight_store(k).start()
        return carry

    late = chunks - 4
    lax.fori_loop(0, late, average, 0)

    def back_arrived(s, carry):
        owner = behind(s)
        pltpu.make_async_remote_copy(
            src_ref=cotangent_out.at[owner],
            dst_ref=cotangent_in.at[hidden_rows(owner)],
            send_sem=back_send.at[s],
            recv_sem=back_recv.at[s],
            device_id=(replica, owner),
            device_id_type=MESH,
        ).wait_recv()
        return carry

    lax.fori_loop(1, GROUP, back_arrived, 0)

    def turn_back(b, carry):
        for t in range(TURNS):
            lanes = pl.ds(pl.multiple_of((b * TURNS + t) * LANES, LANES), LANES)
            block = cotangent_in[lanes, :].T
            token_hidden[:, :, lanes] = block.reshape(micro, tokens, LANES)
        return carry

    lax.fori_loop(0, blocks // TURNS, turn_back, 0)
    hidden_grad_store = pltpu.make_async_copy(token_hidden, hidden_grad_hbm.at[0], load_sem.at[0])
    hidden_grad_store.start()

    lax.fori_loop(late, chunks, average, 0)

    def sent(k, carry):
        gather_copy(k, TO_X, unit_rows(z, core, x_hi), x_peer).wait_send()
        gather_copy(k, TO_NEXT, pair_rows(z, core), next_peer).wait_send()
        gather_copy(k, TO_PREV, pair_rows(z, core), prev_peer).wait_send()
        gather_copy(k, CORE_OWN, pair_rows(z, core), core_peer).wait_send()
        gather_copy(k, ON_NEXT, unit_rows(z_prev, core, 0), next_peer).wait_send()
        gather_copy(k, ON_PREV, unit_rows(z_next, core, 1), prev_peer).wait_send()
        gather_copy(k, CORE_PREV, pair_rows(z_prev, core), core_peer).wait_send()
        gather_copy(k, CORE_NEXT, pair_rows(z_next, core), core_peer).wait_send()
        gather_copy(k, CORE_FAR, pair_rows(z_far, core), core_peer).wait_send()
        gossip_copy(k).wait_send()
        weight_store(k).wait()
        return carry

    lax.fori_loop(0, chunks, sent, 0)

    def exchanged(s, carry):
        hidden_copy(s).wait_send()
        back_copy(s).wait_send()
        return carry

    lax.fori_loop(1, GROUP, exchanged, 0)
    for k in (chunks - 2, chunks - 1):
        moment_store(k).wait()
    if relays:

        @pl.when(lands | wraps)
        def _():
            def passed(j, carry):
                pass_on_copy(j, x_beside).wait_send()
                return carry

            lax.fori_loop(0, relays, passed, 0)

    hidden_grad_store.wait()


def step_call(level, factor, scale, hidden, out_grad, weight, moment, second):
    _, micro, tokens, width = hidden.shape
    _, rows, depth = weight.shape
    chunks = depth // CHUNK
    unit = micro * tokens
    relays = chunks // 2
    half = jnp.bfloat16
    anywhere = pl.BlockSpec(memory_space=pl.ANY)
    scratch = [
        pltpu.VMEM((chunks, GROUP * unit, CHUNK), half),
        pltpu.VMEM((micro, tokens, width), half),
        pltpu.VMEM((width, unit), half),
        pltpu.VMEM((GROUP, rows, unit), half),
        pltpu.VMEM((rows, GROUP * unit), half),
        pltpu.VMEM((rows, GROUP * unit), jnp.float32),
        pltpu.VMEM((chunks, rows, CHUNK), half),
        pltpu.VMEM((chunks, rows, CHUNK), half),
        pltpu.VMEM((GROUP, rows, unit), half),
        pltpu.VMEM((width, unit), half),
        pltpu.VMEM((2, rows, CHUNK), half),
        pltpu.VMEM((2, rows, CHUNK), half),
        pltpu.VMEM((2, rows, CHUNK), half),
        pltpu.VMEM((2, rows, CHUNK), half),
        pltpu.VMEM((relays, rows, CHUNK), half),
        pltpu.SemaphoreType.DMA((1,)),
        pltpu.SemaphoreType.DMA((chunks, micro)),
        pltpu.SemaphoreType.DMA((2, 3)),
        pltpu.SemaphoreType.DMA((2,)),
        pltpu.SemaphoreType.DMA((chunks,)),
        pltpu.SemaphoreType.DMA((chunks, COPIES)),
        pltpu.SemaphoreType.DMA((chunks, COPIES)),
        pltpu.SemaphoreType.DMA((GROUP,)),
        pltpu.SemaphoreType.DMA((GROUP,)),
        pltpu.SemaphoreType.DMA((GROUP,)),
        pltpu.SemaphoreType.DMA((GROUP,)),
        pltpu.SemaphoreType.DMA((chunks,)),
        pltpu.SemaphoreType.DMA((chunks,)),
        pltpu.SemaphoreType.DMA((relays,)),
        pltpu.SemaphoreType.DMA((relays,)),
    ]
    products = 2 * GROUP * unit * rows * depth
    return pl.pallas_call(
        functools.partial(step_kernel, 1 << level, factor),
        out_shape=(
            jax.ShapeDtypeStruct(weight.shape, half),
            jax.ShapeDtypeStruct(moment.shape, half),
            jax.ShapeDtypeStruct(hidden.shape, half),
        ),
        in_specs=[pl.BlockSpec(memory_space=pltpu.SMEM)] + [anywhere] * 5,
        out_specs=(anywhere,) * 3,
        scratch_shapes=scratch,
        name=f"step_{1 << level}",
        cost_estimate=pl.CostEstimate(
            flops=2 * products,
            bytes_accessed=2 * (2 * hidden.size + out_grad.size + 5 * weight.size),
            transcendentals=weight.size,
        ),
        compiler_params=pltpu.CompilerParams(
            collective_id=level, has_side_effects=True, vmem_limit_bytes=50 * 2**20
        ),
    )(scale, hidden, out_grad, weight, moment, second)


def on_device(step_index, hidden, out_grad, weight, moment, second):
    factor = hidden.shape[3] ** (-0.5)
    step_float = step_index.astype(jnp.float32)
    scale = jnp.stack([1.0 - beta_one**step_float, 1.0 - beta_two**step_float])
    levels = REPLICAS.bit_length() - 1
    branches = [functools.partial(step_call, level, factor) for level in range(levels)]
    return lax.switch(
        step_index % levels, branches, scale, hidden, out_grad, weight, moment, second
    )


def solution(mesh):
    placed = (
        P(),
        P("replica", None, "fsdp", None),
        P("replica", None, "fsdp", None),
        P("replica", "fsdp", None),
        P("replica", "fsdp", None),
        P("replica", "fsdp", None),
    )
    return jax.shard_map(
        on_device,
        mesh=mesh,
        in_specs=placed,
        out_specs=(
            P("replica", "fsdp", None),
            P("replica", "fsdp", None),
            P("replica", None, "fsdp", None),
        ),
        check_vma=False,
    )
```

```python
import functools

import jax
import jax.numpy as jnp
from jax import lax
from jax.experimental import pallas as pl
from jax.experimental.pallas import tpu as pltpu
from jax.sharding import PartitionSpec as P

beta_one = 0.9
beta_two = 0.95
learn_rate = 0.05
decay_rate = 0.4
epsilon = 1e-08

MESH = pl.DeviceIdType.MESH
GROUP = 16
REPLICAS = 8
LANES = 128
CHUNK = 256
EARLY = 8
FORWARD, FAR, USE, RELAY = 2, 4, 5, 8
TURNS = 6

TO_X, TO_NEXT, TO_PREV, CORE_OWN, ON_NEXT, ON_PREV, CORE_PREV, CORE_NEXT, CORE_FAR = range(9)
COPIES = 9


def slot_of(index):
    x_hi, z, core = index // 8, (index // 2) % 4, index % 2
    return z * 4 + core * 2 + x_hi


def step_kernel(
    distance,
    factor,
    scale_ref,
    hidden_hbm,
    grads_hbm,
    weight_hbm,
    moment_hbm,
    second_hbm,
    new_weight_hbm,
    new_moment_hbm,
    hidden_grad_hbm,
    gathered,
    token_hidden,
    hidden_out,
    hidden_in,
    hidden_t,
    total,
    stepped,
    partner,
    cotangent_out,
    cotangent_in,
    weight_buf,
    moment_buf,
    second_buf,
    new_moment_buf,
    relayed,
    load_sem,
    own_sem,
    param_sem,
    moment_out_sem,
    weight_out_sem,
    gather_send,
    gather_recv,
    hidden_send,
    hidden_recv,
    back_send,
    back_recv,
    gossip_send,
    gossip_recv,
    relay_send,
    relay_recv,
):
    chunks = gathered.shape[0]
    rows = weight_buf.shape[1]
    micro, tokens = token_hidden.shape[0], token_hidden.shape[1]
    width = token_hidden.shape[2]
    unit = micro * tokens
    blocks = width // LANES

    replica = lax.axis_index("replica")
    index = lax.axis_index("fsdp")
    x_hi, z, core = index // 8, (index // 2) % 4, index % 2
    z_next, z_prev, z_far = (z + 1) % 4, (z + 3) % 4, (z + 2) % 4

    def place(x, zz, c):
        return (replica, (x * 4 + zz) * 2 + c)

    x_peer = place(1 - x_hi, z, core)
    next_peer = place(x_hi, z_next, core)
    prev_peer = place(x_hi, z_prev, core)
    core_peer = place(x_hi, z, 1 - core)
    gossip_to = ((replica + distance) % REPLICAS, index)
    gossip_from = ((replica + REPLICAS - distance) % REPLICAS, index)

    x_lo, y = replica // 4, replica % 4
    relays = relayed.shape[0] if distance < 4 else 0
    wraps = y >= 4 - distance
    lands = y < distance
    y_ahead = (x_lo * 4 + (y + distance) % 4, index)
    y_behind = (x_lo * 4 + (y + 4 - distance) % 4, index)
    x_beside = ((1 - x_lo) * 4 + y, index)

    def pair_rows(zz, c):
        return pl.ds(pl.multiple_of((zz * 2 + c) * 2 * unit, 2 * unit), 2 * unit)

    def unit_rows(zz, c, x):
        return pl.ds(pl.multiple_of((zz * 4 + c * 2 + x) * unit, unit), unit)

    def chunk_columns(k):
        return pl.ds(pl.multiple_of(k * CHUNK, CHUNK), CHUNK)

    hidden_load = pltpu.make_async_copy(hidden_hbm.at[0], token_hidden, load_sem.at[0])
    hidden_load.start()

    own_start = slot_of(index) * unit

    def own_load(k, part):
        return pltpu.make_async_copy(
            grads_hbm.at[0, part, :, chunk_columns(k)],
            gathered.at[k, pl.ds(pl.multiple_of(own_start + part * tokens, tokens), tokens)],
            own_sem.at[k, part],
        )

    def start_own(k, carry):
        for part in range(micro):
            own_load(k, part).start()
        return carry

    lax.fori_loop(0, chunks, start_own, 0)

    def param_loads(k):
        slot = k % 2
        return [
            pltpu.make_async_copy(
                source.at[0, :, chunk_columns(k)], target.at[slot], param_sem.at[slot, i]
            )
            for i, (source, target) in enumerate(
                (
                    (weight_hbm, weight_buf),
                    (moment_hbm, moment_buf),
                    (second_hbm, second_buf),
                )
            )
        ]

    for load in param_loads(0):
        load.start()

    barrier = pltpu.get_barrier_semaphore()

    def greet(s, carry):
        pl.semaphore_signal(
            barrier, 1, device_id=(replica, (index + s) % GROUP), device_id_type=MESH
        )
        return carry

    lax.fori_loop(1, GROUP, greet, 0)
    pl.semaphore_signal(barrier, 1, device_id=gossip_to, device_id_type=MESH)
    pl.semaphore_signal(barrier, 1, device_id=gossip_from, device_id_type=MESH)
    greeted = GROUP - 1 + 2
    if relays:
        for peer in (y_ahead, y_behind, x_beside):
            pl.semaphore_signal(barrier, 1, device_id=peer, device_id_type=MESH)
        greeted += 3
    pl.semaphore_wait(barrier, greeted)

    def gather_copy(k, which, where, peer):
        return pltpu.make_async_remote_copy(
            src_ref=gathered.at[k, where],
            dst_ref=gathered.at[k, where],
            send_sem=gather_send.at[k, which],
            recv_sem=gather_recv.at[k, which],
            device_id=peer,
            device_id_type=MESH,
        )

    def stage_x(k):
        for part in range(micro):
            own_load(k, part).wait()
        gather_copy(k, TO_X, unit_rows(z, core, x_hi), x_peer).start()

    def stage_pair(k):
        gather_copy(k, TO_X, unit_rows(z, core, 1 - x_hi), x_peer).wait_recv()
        gather_copy(k, TO_NEXT, pair_rows(z, core), next_peer).start()
        gather_copy(k, TO_PREV, pair_rows(z, core), prev_peer).start()
        gather_copy(k, CORE_OWN, pair_rows(z, core), core_peer).start()

    def stage_forward(k):
        gather_copy(k, TO_NEXT, pair_rows(z_prev, core), next_peer).wait_recv()
        gather_copy(k, ON_NEXT, unit_rows(z_prev, core, 0), next_peer).start()
        gather_copy(k, TO_PREV, pair_rows(z_next, core), prev_peer).wait_recv()
        gather_copy(k, ON_PREV, unit_rows(z_next, core, 1), prev_peer).start()
        gather_copy(k, CORE_PREV, pair_rows(z_prev, core), core_peer).start()
        gather_copy(k, CORE_NEXT, pair_rows(z_next, core), core_peer).start()

    def stage_far(k):
        gather_copy(k, ON_NEXT, unit_rows(z_far, core, 0), next_peer).wait_recv()
        gather_copy(k, ON_PREV, unit_rows(z_far, core, 1), prev_peer).wait_recv()
        gather_copy(k, CORE_FAR, pair_rows(z_far, core), core_peer).start()

    def stage_core(k):
        for which, zz in (
            (CORE_OWN, z),
            (CORE_PREV, z_prev),
            (CORE_NEXT, z_next),
            (CORE_FAR, z_far),
        ):
            gather_copy(k, which, pair_rows(zz, 1 - core), core_peer).wait_recv()

    stage_x(0)
    stage_x(1)

    hidden_load.wait()

    def turn(b, carry):
        for t in range(TURNS):
            lanes = pl.ds(pl.multiple_of((b * TURNS + t) * LANES, LANES), LANES)
            block = token_hidden[:, :, lanes].reshape(unit, LANES)
            hidden_out[lanes, :] = block.T
        return carry

    lax.fori_loop(0, blocks // TURNS, turn, 0)

    def ahead(s):
        return ((x_hi + s // 8) % 2 * 4 + (z + (s // 2) % 4) % 4) * 2 + (core + s) % 2

    def behind(s):
        return ((x_hi + s // 8) % 2 * 4 + (z + 4 - (s // 2) % 4) % 4) * 2 + (core + s) % 2

    def hidden_rows(f):
        return pl.ds(pl.multiple_of(f * rows, 16), rows)

    def hidden_copy(s):
        peer = ahead(s)
        return pltpu.make_async_remote_copy(
            src_ref=hidden_out.at[hidden_rows(peer)],
            dst_ref=hidden_in.at[slot_of(index)],
            send_sem=hidden_send.at[s],
            recv_sem=hidden_recv.at[s],
            device_id=(replica, peer),
            device_id_type=MESH,
        )

    def hidden_start(s, carry):
        hidden_copy(GROUP - s).start()
        return carry

    lax.fori_loop(1, GROUP, hidden_start, 0)

    def exchange(k, carry):
        stage_x(k)
        return carry

    lax.fori_loop(2, EARLY, exchange, 0)

    def hidden_arrived(s, carry):
        owner = behind(s)
        slot = slot_of(owner)
        pltpu.make_async_remote_copy(
            src_ref=hidden_out.at[hidden_rows(index)],
            dst_ref=hidden_in.at[slot],
            send_sem=hidden_send.at[s],
            recv_sem=hidden_recv.at[s],
            device_id=(replica, owner),
            device_id_type=MESH,
        ).wait_recv()
        lanes = pl.ds(pl.multiple_of(slot * unit, unit), unit)
        hidden_t[:, lanes] = hidden_in[slot]
        return carry

    def gossip_copy(k):
        return pltpu.make_async_remote_copy(
            src_ref=stepped.at[k],
            dst_ref=partner.at[k],
            send_sem=gossip_send.at[k],
            recv_sem=gossip_recv.at[k],
            device_id=gossip_to,
            device_id_type=MESH,
        )

    def relay_copy(k, peer):
        return pltpu.make_async_remote_copy(
            src_ref=stepped.at[k],
            dst_ref=relayed.at[k % relays],
            send_sem=gossip_send.at[k],
            recv_sem=relay_recv.at[k % relays],
            device_id=peer,
            device_id_type=MESH,
        )

    def pass_on_copy(k, peer):
        return pltpu.make_async_remote_copy(
            src_ref=relayed.at[k % relays],
            dst_ref=partner.at[k],
            send_sem=relay_send.at[k % relays],
            recv_sem=gossip_recv.at[k],
            device_id=peer,
            device_id_type=MESH,
        )

    def pass_on(k, peer):
        relay_copy(k, x_beside).wait_recv()
        pass_on_copy(k, peer).start()

    def gossip_start(k):
        if relays:

            @pl.when(wraps & (k < relays))
            def _():
                relay_copy(k, y_ahead).start()

            @pl.when(wraps & (k >= relays))
            def _():
                relay_copy(k, x_beside).start()

            @pl.when(jnp.logical_not(wraps))
            def _():
                gossip_copy(k).start()

        else:
            gossip_copy(k).start()

    def moment_store(k):
        return pltpu.make_async_copy(
            new_moment_buf.at[k % 2],
            new_moment_hbm.at[0, :, chunk_columns(k)],
            moment_out_sem.at[k % 2],
        )

    def weight_store(k):
        return pltpu.make_async_copy(
            partner.at[k],
            new_weight_hbm.at[0, :, chunk_columns(k)],
            weight_out_sem.at[k],
        )

    bias_one = scale_ref[0]
    bias_two = scale_ref[1]

    def update(k):
        slot = k % 2
        for load in param_loads(k):
            load.wait()

        @pl.when(k + 1 < chunks)
        def _():
            for load in param_loads(k + 1):
                load.start()

        gradient = factor * jnp.dot(
            hidden_t[...], gathered[k], preferred_element_type=jnp.float32
        )

        @pl.when(k >= 2)
        def _():
            moment_store(k - 2).wait()

        first = beta_one * moment_buf[slot].astype(jnp.float32) + (1.0 - beta_one) * gradient
        new_moment_buf[slot] = first.astype(jnp.bfloat16)
        variance = (
            beta_two * second_buf[slot].astype(jnp.float32)
            + (1.0 - beta_two) * gradient * gradient
        )
        change = first / bias_one / (jnp.sqrt(variance / bias_two) + epsilon)
        wide = weight_buf[slot].astype(jnp.float32)
        stepped[k] = (wide - learn_rate * (change + decay_rate * wide)).astype(jnp.bfloat16)
        gossip_start(k)
        moment_store(k).start()

    def cotangent(k):
        slot = k % 2
        part = lax.dot_general(
            weight_buf[slot],
            gathered[k],
            (((1,), (1,)), ((), ())),
            preferred_element_type=jnp.float32,
        )
        total[...] += part

    def step(i, carry):
        @pl.when(i < chunks)
        def _():
            stage_pair(i)

        @pl.when((i >= FORWARD) & (i - FORWARD < chunks))
        def _():
            stage_forward(i - FORWARD)

        @pl.when(i == USE)
        def _():
            lax.fori_loop(1, GROUP, hidden_arrived, 0)
            own_lanes = pl.ds(pl.multiple_of(slot_of(index) * unit, unit), unit)
            hidden_t[:, own_lanes] = hidden_out[hidden_rows(index)]
            total[...] = jnp.zeros_like(total)
            lax.fori_loop(EARLY, chunks, exchange, 0)

        @pl.when((i >= USE) & (i - USE < chunks))
        def _():
            stage_core(i - USE)
            update(i - USE)

        @pl.when((i >= FAR) & (i - FAR < chunks))
        def _():
            stage_far(i - FAR)

        @pl.when((i >= USE) & (i - USE < chunks))
        def _():
            cotangent(i - USE)

        if relays:
            over_y, over_x = i - RELAY, i - USE - 1

            @pl.when(lands & (over_y >= 0) & (over_y < relays))
            def _():
                pass_on(over_y, x_beside)

            @pl.when(wraps & (over_x >= relays))
            def _():
                pass_on(over_x, y_ahead)

        return carry

    lax.fori_loop(0, chunks + USE, step, 0)

    def back_copy(s):
        peer = ahead(s)
        return pltpu.make_async_remote_copy(
            src_ref=cotangent_out.at[peer],
            dst_ref=cotangent_in.at[hidden_rows(index)],
            send_sem=back_send.at[s],
            recv_sem=back_recv.at[s],
            device_id=(replica, peer),
            device_id_type=MESH,
        )

    def part_of(f):
        lanes = pl.ds(pl.multiple_of(slot_of(f) * unit, unit), unit)
        return (factor * total[:, lanes]).astype(jnp.bfloat16)

    def back_start(s, carry):
        peer = ahead(GROUP - s)
        cotangent_out[peer] = part_of(peer)
        back_copy(GROUP - s).start()
        return carry

    lax.fori_loop(1, GROUP, back_start, 0)
    cotangent_in[hidden_rows(index)] = part_of(index)
    if relays:

        @pl.when(wraps)
        def _():
            pass_on(chunks - 1, y_ahead)


    def average(k, carry):
        gossip_copy(k).wait_recv()
        mean = 0.5 * (stepped[k].astype(jnp.float32) + partner[k].astype(jnp.float32))
        partner[k] = mean.astype(jnp.bfloat16)
        weight_store(k).start()
        return carry

    late = chunks - 4
    lax.fori_loop(0, late, average, 0)

    def back_arrived(s, carry):
        owner = behind(s)
        pltpu.make_async_remote_copy(
            src_ref=cotangent_out.at[owner],
            dst_ref=cotangent_in.at[hidden_rows(owner)],
            send_sem=back_send.at[s],
            recv_sem=back_recv.at[s],
            device_id=(replica, owner),
            device_id_type=MESH,
        ).wait_recv()
        return carry

    lax.fori_loop(1, GROUP, back_arrived, 0)

    def turn_back(b, carry):
        for t in range(TURNS):
            lanes = pl.ds(pl.multiple_of((b * TURNS + t) * LANES, LANES), LANES)
            block = cotangent_in[lanes, :].T
            token_hidden[:, :, lanes] = block.reshape(micro, tokens, LANES)
        return carry

    lax.fori_loop(0, blocks // TURNS, turn_back, 0)
    hidden_grad_store = pltpu.make_async_copy(token_hidden, hidden_grad_hbm.at[0], load_sem.at[0])
    hidden_grad_store.start()

    lax.fori_loop(late, chunks, average, 0)

    def sent(k, carry):
        gather_copy(k, TO_X, unit_rows(z, core, x_hi), x_peer).wait_send()
        gather_copy(k, TO_NEXT, pair_rows(z, core), next_peer).wait_send()
        gather_copy(k, TO_PREV, pair_rows(z, core), prev_peer).wait_send()
        gather_copy(k, CORE_OWN, pair_rows(z, core), core_peer).wait_send()
        gather_copy(k, ON_NEXT, unit_rows(z_prev, core, 0), next_peer).wait_send()
        gather_copy(k, ON_PREV, unit_rows(z_next, core, 1), prev_peer).wait_send()
        gather_copy(k, CORE_PREV, pair_rows(z_prev, core), core_peer).wait_send()
        gather_copy(k, CORE_NEXT, pair_rows(z_next, core), core_peer).wait_send()
        gather_copy(k, CORE_FAR, pair_rows(z_far, core), core_peer).wait_send()
        gossip_copy(k).wait_send()
        weight_store(k).wait()
        return carry

    lax.fori_loop(0, chunks, sent, 0)

    def exchanged(s, carry):
        hidden_copy(s).wait_send()
        back_copy(s).wait_send()
        return carry

    lax.fori_loop(1, GROUP, exchanged, 0)
    for k in (chunks - 2, chunks - 1):
        moment_store(k).wait()
    if relays:

        def passed(j, carry):
            pass_on_copy(j, x_beside).wait_send()
            return carry

        @pl.when(lands)
        def _():
            lax.fori_loop(0, relays, passed, 0)

        @pl.when(wraps)
        def _():
            lax.fori_loop(relays, chunks, passed, 0)

    hidden_grad_store.wait()


def step_call(level, factor, scale, hidden, out_grad, weight, moment, second):
    _, micro, tokens, width = hidden.shape
    _, rows, depth = weight.shape
    chunks = depth // CHUNK
    unit = micro * tokens
    relays = chunks * 15 // 20
    half = jnp.bfloat16
    anywhere = pl.BlockSpec(memory_space=pl.ANY)
    scratch = [
        pltpu.VMEM((chunks, GROUP * unit, CHUNK), half),
        pltpu.VMEM((micro, tokens, width), half),
        pltpu.VMEM((width, unit), half),
        pltpu.VMEM((GROUP, rows, unit), half),
        pltpu.VMEM((rows, GROUP * unit), half),
        pltpu.VMEM((rows, GROUP * unit), jnp.float32),
        pltpu.VMEM((chunks, rows, CHUNK), half),
        pltpu.VMEM((chunks, rows, CHUNK), half),
        pltpu.VMEM((GROUP, rows, unit), half),
        pltpu.VMEM((width, unit), half),
        pltpu.VMEM((2, rows, CHUNK), half),
        pltpu.VMEM((2, rows, CHUNK), half),
        pltpu.VMEM((2, rows, CHUNK), half),
        pltpu.VMEM((2, rows, CHUNK), half),
        pltpu.VMEM((relays, rows, CHUNK), half),
        pltpu.SemaphoreType.DMA((1,)),
        pltpu.SemaphoreType.DMA((chunks, micro)),
        pltpu.SemaphoreType.DMA((2, 3)),
        pltpu.SemaphoreType.DMA((2,)),
        pltpu.SemaphoreType.DMA((chunks,)),
        pltpu.SemaphoreType.DMA((chunks, COPIES)),
        pltpu.SemaphoreType.DMA((chunks, COPIES)),
        pltpu.SemaphoreType.DMA((GROUP,)),
        pltpu.SemaphoreType.DMA((GROUP,)),
        pltpu.SemaphoreType.DMA((GROUP,)),
        pltpu.SemaphoreType.DMA((GROUP,)),
        pltpu.SemaphoreType.DMA((chunks,)),
        pltpu.SemaphoreType.DMA((chunks,)),
        pltpu.SemaphoreType.DMA((relays,)),
        pltpu.SemaphoreType.DMA((relays,)),
    ]
    products = 2 * GROUP * unit * rows * depth
    return pl.pallas_call(
        functools.partial(step_kernel, 1 << level, factor),
        out_shape=(
            jax.ShapeDtypeStruct(weight.shape, half),
            jax.ShapeDtypeStruct(moment.shape, half),
            jax.ShapeDtypeStruct(hidden.shape, half),
        ),
        in_specs=[pl.BlockSpec(memory_space=pltpu.SMEM)] + [anywhere] * 5,
        out_specs=(anywhere,) * 3,
        scratch_shapes=scratch,
        name=f"step_{1 << level}",
        cost_estimate=pl.CostEstimate(
            flops=2 * products,
            bytes_accessed=2 * (2 * hidden.size + out_grad.size + 5 * weight.size),
            transcendentals=weight.size,
        ),
        compiler_params=pltpu.CompilerParams(
            collective_id=level, has_side_effects=True, vmem_limit_bytes=50 * 2**20
        ),
    )(scale, hidden, out_grad, weight, moment, second)


def on_device(step_index, hidden, out_grad, weight, moment, second):
    factor = hidden.shape[3] ** (-0.5)
    step_float = step_index.astype(jnp.float32)
    scale = jnp.stack([1.0 - beta_one**step_float, 1.0 - beta_two**step_float])
    levels = REPLICAS.bit_length() - 1
    branches = [functools.partial(step_call, level, factor) for level in range(levels)]
    return lax.switch(
        step_index % levels, branches, scale, hidden, out_grad, weight, moment, second
    )


def solution(mesh):
    placed = (
        P(),
        P("replica", None, "fsdp", None),
        P("replica", None, "fsdp", None),
        P("replica", "fsdp", None),
        P("replica", "fsdp", None),
        P("replica", "fsdp", None),
    )
    return jax.shard_map(
        on_device,
        mesh=mesh,
        in_specs=placed,
        out_specs=(
            P("replica", "fsdp", None),
            P("replica", "fsdp", None),
            P("replica", None, "fsdp", None),
        ),
        check_vma=False,
    )
```
